32 devices in a mesh: sa: 4 (over z), sb: 8 (over y, x, core).
Axes of the slice: x: 2, y: 2, z: 4, core: 2. Of those that a mesh axis runs over, the one named last changes fastest.
Arguments:
- queries: float32 [8192, 128], P(('sa', 'sb')), may hold values from -6 to 6
- keys: float32 [8192, 128], P(('sa', 'sb')), may hold values from -6 to 6
- values: float32 [8192, 128], P(('sa', 'sb')), may hold values from -6 to 6
- cotangent: float32 [8192, 128], P(('sa', 'sb')), may hold values from -6 to 6
- filt: float32 [8192, 128], P(('sa', 'sb')), may hold values from -6 to 6
- skip: float32 [128], replicated, may hold values from -4 to 4
Outputs:
- grad_queries: float32 [8192, 128], P(('sa', 'sb'))
- grad_keys: float32 [8192, 128], P(('sa', 'sb'))
- grad_values: float32 [8192, 128], P(('sa', 'sb'))
- grad_filter: float32 [8192, 128], P(('sa', 'sb'))
The draws below stay inside these ranges and needn't reach their ends.
All inputs are finite; a program needn't handle non-finite values.
Results may differ from the reference program's by a relative error of at most 0.000098.
Values sent between devices are 32-bit elements; how exact they have to be, the bound alone decides.
No kernel may reach another device: no remote copies, remote signals or barrier semaphores. Data moves between devices by JAX's collectives and lax.ppermute only.
A program may use at most 64 MiB of HBM per device.

```python
import jax
import jax.numpy as jnp

CH = 128
TOKENS = 8192


def shard_levels(stream_key, dims, pieces, least, top_value):
    def one(axis_at, parts):
        draws = jax.random.uniform(jax.random.fold_in(jax.random.fold_in(stream_key, 6), axis_at), (parts,), jnp.float32, least / len(pieces), top_value / len(pieces))
        return jnp.repeat(jnp.exp(draws), dims[axis_at] // parts).reshape((-1,) + (1,) * (len(dims) - axis_at - 1))

    loudness = one(*pieces[0])
    for cut in pieces[1:]:
        loudness = loudness * one(*cut)
    return loudness


def noise(key, extent, spread, most, split=(), kind=jnp.bfloat16):
    values = jax.random.normal(key, extent, jnp.float32) * spread
    if len(split) > 0:
        values = shard_levels(key, extent, split, -0.22, 0.18) * values
    return jnp.clip(values, min=-most, max=most).astype(kind)


def setup_inputs(seed: int = 0) -> dict:
    arg_keys = jax.random.split(jax.random.key(seed), 7)
    return {
        "queries": noise(arg_keys[0], (TOKENS, CH), 1.0, 6.0, ((0, 32),), jnp.float32),
        "keys": noise(arg_keys[1], (TOKENS, CH), 1.0, 6.0, ((0, 32),), jnp.float32),
        "values": noise(arg_keys[2], (TOKENS, CH), 1.0, 6.0, ((0, 32),), jnp.float32),
        "cotangent": noise(arg_keys[3], (TOKENS, CH), 1.0, 6.0, ((0, 32),), jnp.float32),
        "filt": noise(arg_keys[4], (TOKENS, CH), 1.0, 6.0, ((0, 32),), jnp.float32),
        "skip": noise(arg_keys[5], (CH,), 1.0, 4.0, (), jnp.float32),
    }


def reference(queries, keys, values, cotangent, filt, skip):
    tokens = queries.shape[0]
    scaling = 1.0 / jnp.sqrt(jnp.float32(tokens))
    gated = keys * values
    upstream = cotangent * queries
    padded = 2 * tokens
    spectrum_gated = jnp.fft.fft(gated, n=padded, axis=0)
    spectrum_filter = jnp.fft.fft(filt, n=padded, axis=0)
    spectrum_upstream = jnp.fft.fft(upstream, n=padded, axis=0)
    conv_part = jnp.real(jnp.fft.ifft(spectrum_filter * spectrum_gated, axis=0))[:tokens]
    response = conv_part * scaling + skip * gated
    back_part = jnp.real(jnp.fft.ifft(jnp.conj(spectrum_filter) * spectrum_upstream, axis=0))[:tokens]
    back_signal = back_part * scaling + skip * upstream
    filter_part = jnp.real(jnp.fft.ifft(jnp.conj(spectrum_gated) * spectrum_upstream, axis=0))[:tokens]
    grad_filter = filter_part * scaling
    return (cotangent * response, back_signal * values, back_signal * keys, grad_filter)
```

```python
import math

import jax
import jax.numpy as jnp
import ml_dtypes
import numpy as np
from jax import lax
from jax.experimental import pallas as pl
from jax.experimental.pallas import tpu as pltpu
from jax.sharding import PartitionSpec as P

LANES = 128
AXES = ("sa", "sb")
VMEM_LIMIT = 48 * 1024 * 1024


def halves(matrix):
    high = matrix.astype(ml_dtypes.bfloat16)
    low = (matrix - high.astype(np.float64)).astype(ml_dtypes.bfloat16)
    return high, low


def tables(tokens, devices):
    rows = tokens // LANES
    parts = rows // devices
    order = np.arange(rows).reshape(devices, parts).T.reshape(-1)
    half_step = np.arange(rows) + 0.5
    lane = np.arange(LANES)
    angle = 2.0 * np.pi / (2 * rows) * half_step[:, None] * order[None, :]
    first = np.concatenate([np.cos(angle), -np.sin(angle)], axis=0)
    turn_angle = 2.0 * np.pi / (2 * tokens) * half_step[:, None] * lane[None, :]
    turn = np.stack([np.cos(turn_angle), -np.sin(turn_angle)]).astype(np.float32)
    lane_angle = 2.0 * np.pi / LANES * ((lane[:, None] * lane[None, :]) % LANES)
    cosine, sine = np.cos(lane_angle), np.sin(lane_angle)
    second = np.block([[cosine, -sine], [sine, cosine]])
    factor = 1.0 / (tokens * math.sqrt(tokens))
    last = np.concatenate([np.cos(angle).T, np.sin(angle).T], axis=1) * factor
    first_high, first_low = halves(first)
    last_high, last_low = halves(last)
    second_high, second_low = halves(second)
    return (
        np.concatenate([first_high, first_high, first_low], axis=1),
        turn,
        np.stack([second_high, second_low]),
        np.concatenate([last_high, last_high, last_low], axis=1),
    )


def split(array):
    scaled = array * 65537.0
    high = scaled - (scaled - array)
    return high, array - high


def stacked(array):
    high, low = split(array)
    return jnp.concatenate([high, low, high], axis=0)


def matmul(left, right):
    return jnp.dot(left, right, preferred_element_type=jnp.float32)


def gate_kernel(devices, *refs):
    far = refs[:6]
    out = refs[6]
    near = refs[7:13]
    arrivals = refs[13]
    copies = [
        pltpu.make_async_copy(source, target, arrivals.at[number])
        for number, (source, target) in enumerate(zip(far, near))
    ]
    for copy in copies:
        copy.start()
    skip, filt, keys, values, cotangent, queries = near
    segment, channels = queries.shape
    parts = segment // LANES
    share = channels // devices
    block = 3 * parts * share
    for number in (1, 0, 2):
        needed = {0: (2, 3), 1: (0, 1), 2: (4, 5)}[number]
        for index in needed:
            copies[index].wait()
        if number == 1:
            first_tap = jnp.where(lax.axis_index(AXES) == 0, math.sqrt(devices * segment), 0.0)
            filt[0:1, :] += first_tap * skip[...]
        for part in range(parts):
            at = pl.ds(part * LANES, LANES)
            if number == 0:
                signal = keys[at, :] * values[at, :]
            elif number == 1:
                signal = filt[at, :]
            else:
                signal = cotangent[at, :] * queries[at, :]
            turned = signal.T
            for channel in range(share):
                row = (number * parts + part) * share + channel
                out[pl.ds(row, devices, stride=block), :] = turned[
                    channel * devices : (channel + 1) * devices, :
                ]


def conv_kernel(devices, arrived, first, turn, second, last, out, high, low):
    rows = turn.shape[1]
    parts = rows // devices
    block = arrived.shape[0] // devices
    share = block // (3 * parts)
    turn_real = turn[0]
    turn_imag = turn[1]

    def gathered(number, channel):
        pieces = []
        for part in range(parts):
            row = (number * parts + part) * share + channel
            pieces.append(arrived[pl.ds(row, devices, stride=block), :])
        return jnp.concatenate(pieces, axis=0)

    def hold(number, channel, real, imag):
        at = pl.ds((channel * 3 + number) * rows, rows)
        for value, lanes in ((real, pl.ds(0, LANES)), (imag, pl.ds(LANES, LANES))):
            high[at, lanes], low[at, lanes] = split(value)

    def lanes_transform(channel):
        at = pl.ds(channel * 3 * rows, 3 * rows)
        result = (
            matmul(high[at, :], second[0])
            + matmul(high[at, :], second[1])
            + matmul(low[at, :], second[0])
        )
        pieces = []
        for number in range(3):
            piece = result[number * rows : (number + 1) * rows]
            pieces.append((piece[:, 0:LANES], piece[:, LANES : 2 * LANES]))
        return pieces

    for number in range(3):
        signals = [stacked(gathered(number, channel)) for channel in range(share)]
        spread = matmul(first[...], jnp.concatenate(signals, axis=1))
        for channel in range(share):
            lanes = slice(channel * LANES, (channel + 1) * LANES)
            real = spread[:rows, lanes]
            imag = spread[rows:, lanes]
            hold(
                number,
                channel,
                real * turn_real - imag * turn_imag,
                real * turn_imag + imag * turn_real,
            )
    for channel in range(share):
        (gr, gi), (fr, fi), (ur, ui) = lanes_transform(channel)
        hold(0, channel, fr * gr - fi * gi, -(fr * gi + fi * gr))
        hold(1, channel, fr * ur + fi * ui, fi * ur - fr * ui)
        hold(2, channel, gr * ur + gi * ui, gi * ur - gr * ui)
    turned = [[], [], []]
    for channel in range(share):
        for number, (real, imag) in enumerate(lanes_transform(channel)):
            both = (real * turn_real - imag * turn_imag, real * turn_imag + imag * turn_real)
            turned[number].append(stacked(jnp.concatenate(both, axis=0)))
    for number in range(3):
        result = matmul(last[...], jnp.concatenate(turned[number], axis=1))
        for channel in range(share):
            lanes = slice(channel * LANES, (channel + 1) * LANES)
            for part in range(parts):
                row = (number * parts + part) * share + channel
                out[pl.ds(row, devices, stride=block), :] = result[
                    part * devices : (part + 1) * devices, lanes
                ]


def finish_kernel(devices, arrived, keys, values, cotangent, *refs):
    far = refs[:4]
    near = refs[4:8]
    departures = refs[8]
    grad_queries, grad_keys, grad_values, grad_filter = near
    segment, channels = keys.shape
    parts = segment // LANES
    share = channels // devices
    block = 3 * parts * share
    copies = [
        pltpu.make_async_copy(source, target, departures.at[number])
        for number, (source, target) in enumerate(zip(near, far))
    ]

    def convolved(number, part):
        pieces = []
        for channel in range(share):
            row = (number * parts + part) * share + channel
            pieces.append(arrived[pl.ds(row, devices, stride=block), :])
        return jnp.concatenate(pieces, axis=0).T

    blocks = [pl.ds(part * LANES, LANES) for part in range(parts)]
    for part, at in enumerate(blocks):
        back_signal = convolved(1, part)
        grad_keys[at, :] = back_signal * values[at, :]
        grad_values[at, :] = back_signal * keys[at, :]
    copies[1].start()
    copies[2].start()
    for part, at in enumerate(blocks):
        grad_queries[at, :] = cotangent[at, :] * convolved(0, part)
    copies[0].start()
    for part, at in enumerate(blocks):
        grad_filter[at, :] = convolved(2, part)
    copies[3].start()
    for copy in copies:
        copy.wait()


def call(kernel, devices, out_shape, scratch=(), **specs):
    def bound(*refs):
        kernel(devices, *refs)

    return pl.pallas_call(
        bound,
        out_shape=out_shape,
        scratch_shapes=scratch,
        compiler_params=pltpu.CompilerParams(vmem_limit_bytes=VMEM_LIMIT),
        **specs,
    )


def local(queries, keys, values, cotangent, filt, skip):
    segment, channels = queries.shape
    devices = lax.axis_size(AXES)
    tokens = segment * devices
    rows = tokens // LANES
    share = channels // devices
    block = 3 * (segment // LANES) * share
    flat = pltpu.VMEM((devices * block, LANES), jnp.float32)

    def exchange(array):
        array = array.reshape(devices, block, LANES)
        array = lax.all_to_all(array, AXES, split_axis=0, concat_axis=0, tiled=True)
        return array.reshape(devices * block, LANES)

    whole = pltpu.VMEM((segment, channels), jnp.float32)
    result = jax.ShapeDtypeStruct(whole.shape, whole.dtype)
    far = pl.BlockSpec(memory_space=pltpu.HBM)
    near = pl.BlockSpec(memory_space=pltpu.VMEM)
    operands = (skip.reshape(1, channels), filt, keys, values, cotangent, queries)
    operands = tuple(pltpu.with_memory_space_constraint(array, pltpu.HBM) for array in operands)
    scratch = (pltpu.VMEM((1, channels), jnp.float32),) + (whole,) * 5 + (pltpu.SemaphoreType.DMA((6,)),)
    gate = call(gate_kernel, devices, flat, scratch, in_specs=(far,) * 6)
    arrived = exchange(gate(*operands))
    wide = pltpu.VMEM((3 * share * rows, 2 * LANES), jnp.float32)
    constants = tuple(jnp.asarray(table, jnp.float32) for table in tables(tokens, devices))
    convolved = call(conv_kernel, devices, flat, (wide, wide))(arrived, *constants)
    returned = exchange(convolved)
    finish = call(
        finish_kernel,
        devices,
        (result,) * 4,
        (whole,) * 4 + (pltpu.SemaphoreType.DMA((4,)),),
        in_specs=(near,) * 4,
        out_specs=(far,) * 4,
    )
    return tuple(finish(returned, keys, values, cotangent))


def solution(mesh):
    whole = P(AXES, None)
    return jax.shard_map(
        local,
        mesh=mesh,
        in_specs=(whole,) * 5 + (P(),),
        out_specs=(whole,) * 4,
        check_vma=False,
    )
```

```python
import math

import jax
import jax.numpy as jnp
import ml_dtypes
import numpy as np
from jax import lax
from jax.experimental import pallas as pl
from jax.experimental.pallas import tpu as pltpu
from jax.sharding import PartitionSpec as P

LANES = 128
AXES = ("sa", "sb")
EXCHANGE = ("sb", "sa")
VMEM_LIMIT = 48 * 1024 * 1024


def halves(matrix):
    high = matrix.astype(ml_dtypes.bfloat16)
    low = (matrix - high.astype(np.float64)).astype(ml_dtypes.bfloat16)
    return high, low


def tables(tokens, devices, planes):
    rows = tokens // LANES
    parts = rows // devices
    order = np.arange(rows).reshape(planes, devices // planes, parts).transpose(2, 1, 0).reshape(-1)
    half_step = np.arange(rows) + 0.5
    lane = np.arange(LANES)
    angle = 2.0 * np.pi / (2 * rows) * half_step[:, None] * order[None, :]
    first = np.concatenate([np.cos(angle), -np.sin(angle)], axis=0)
    turn_angle = 2.0 * np.pi / (2 * tokens) * half_step[:, None] * lane[None, :]
    turn = np.stack([np.cos(turn_angle), -np.sin(turn_angle)]).astype(np.float32)
    lane_angle = 2.0 * np.pi / LANES * ((lane[:, None] * lane[None, :]) % LANES)
    cosine, sine = np.cos(lane_angle), np.sin(lane_angle)
    second = np.block([[cosine, -sine], [sine, cosine]])
    factor = 1.0 / (tokens * math.sqrt(tokens))
    last = np.concatenate([np.cos(angle).T, np.sin(angle).T], axis=1) * factor
    first_high, first_low = halves(first)
    last_high, last_low = halves(last)
    second_high, second_low = halves(second)
    return (
        np.concatenate([first_high, first_high, first_low], axis=1),
        turn,
        np.stack([second_high, second_low]),
        np.concatenate([last_high, last_high, last_low], axis=1),
    )


def split(array):
    high = array.astype(jnp.bfloat16)
    low = (array - high.astype(jnp.float32)).astype(jnp.bfloat16)
    return high, low


def stacked(array):
    high, low = split(array)
    return jnp.concatenate([high, low, high], axis=0)


def matmul(left, right):
    return jnp.dot(left, right, preferred_element_type=jnp.float32)


def gate_kernel(devices, *refs):
    far = refs[:6]
    out = refs[6]
    near = refs[7:13]
    arrivals = refs[13]
    copies = [
        pltpu.make_async_copy(source, target, arrivals.at[number])
        for number, (source, target) in enumerate(zip(far, near))
    ]
    for copy in copies:
        copy.start()
    skip, filt, keys, values, cotangent, queries = near
    segment, channels = queries.shape
    parts = segment // LANES
    share = channels // devices
    block = 3 * parts * share
    for number in (1, 0, 2):
        needed = {0: (2, 3), 1: (0, 1), 2: (4, 5)}[number]
        for index in needed:
            copies[index].wait()
        if number == 1:
            first_tap = jnp.where(lax.axis_index(AXES) == 0, math.sqrt(devices * segment), 0.0)
            filt[0:1, :] += first_tap * skip[...]
        for part in range(parts):
            at = pl.ds(part * LANES, LANES)
            if number == 0:
                signal = keys[at, :] * values[at, :]
            elif number == 1:
                signal = filt[at, :]
            else:
                signal = cotangent[at, :] * queries[at, :]
            turned = signal.T
            for channel in range(share):
                row = (number * parts + part) * share + channel
                out[pl.ds(row, devices, stride=block), :] = turned[
                    channel * devices : (channel + 1) * devices, :
                ]


def conv_kernel(devices, arrived, first, turn, second, last, out, high, low):
    rows = turn.shape[1]
    parts = rows // devices
    block = arrived.shape[0] // devices
    share = block // (3 * parts)
    turn_real = turn[0]
    turn_imag = turn[1]

    def gathered(number, channel):
        pieces = []
        for part in range(parts):
            row = (number * parts + part) * share + channel
            pieces.append(arrived[pl.ds(row, devices, stride=block), :])
        return jnp.concatenate(pieces, axis=0)

    def hold(number, channel, real, imag):
        at = pl.ds((channel * 3 + number) * rows, rows)
        for value, lanes in ((real, pl.ds(0, LANES)), (imag, pl.ds(LANES, LANES))):
            high[at, lanes], low[at, lanes] = split(value)

    def lanes_transform(channel):
        at = pl.ds(channel * 3 * rows, 3 * rows)
        result = (
            matmul(high[at, :], second[0])
            + matmul(high[at, :], second[1])
            + matmul(low[at, :], second[0])
        )
        pieces = []
        for number in range(3):
            piece = result[number * rows : (number + 1) * rows]
            pieces.append((piece[:, 0:LANES], piece[:, LANES : 2 * LANES]))
        return pieces

    for number in range(3):
        signals = [stacked(gathered(number, channel)) for channel in range(share)]
        spread = matmul(first[...], jnp.concatenate(signals, axis=1))
        for channel in range(share):
            lanes = slice(channel * LANES, (channel + 1) * LANES)
            real = spread[:rows, lanes]
            imag = spread[rows:, lanes]
            hold(
                number,
                channel,
                real * turn_real - imag * turn_imag,
                real * turn_imag + imag * turn_real,
            )
    for channel in range(share):
        (gr, gi), (fr, fi), (ur, ui) = lanes_transform(channel)
        hold(0, channel, fr * gr - fi * gi, -(fr * gi + fi * gr))
        hold(1, channel, fr * ur + fi * ui, fi * ur - fr * ui)
        hold(2, channel, gr * ur + gi * ui, gi * ur - gr * ui)
    turned = [[], [], []]
    for channel in range(share):
        for number, (real, imag) in enumerate(lanes_transform(channel)):
            both = (real * turn_real - imag * turn_imag, real * turn_imag + imag * turn_real)
            turned[number].append(stacked(jnp.concatenate(both, axis=0)))
    for number in range(3):
        result = matmul(last[...], jnp.concatenate(turned[number], axis=1))
        for channel in range(share):
            lanes = slice(channel * LANES, (channel + 1) * LANES)
            for part in range(parts):
                row = (number * parts + part) * share + channel
                out[pl.ds(row, devices, stride=block), :] = result[
                    part * devices : (part + 1) * devices, lanes
                ]


def finish_kernel(devices, arrived, keys, values, cotangent, *refs):
    far = refs[:4]
    near = refs[4:8]
    departures = refs[8]
    grad_queries, grad_keys, grad_values, grad_filter = near
    segment, channels = keys.shape
    parts = segment // LANES
    share = channels // devices
    block = 3 * parts * share
    copies = [
        pltpu.make_async_copy(source, target, departures.at[number])
        for number, (source, target) in enumerate(zip(near, far))
    ]

    def convolved(number, part):
        pieces = []
        for channel in range(share):
            row = (number * parts + part) * share + channel
            pieces.append(arrived[pl.ds(row, devices, stride=block), :])
        return jnp.concatenate(pieces, axis=0).T

    blocks = [pl.ds(part * LANES, LANES) for part in range(parts)]
    for part, at in enumerate(blocks):
        back_signal = convolved(1, part)
        grad_keys[at, :] = back_signal * values[at, :]
        grad_values[at, :] = back_signal * keys[at, :]
    copies[1].start()
    copies[2].start()
    for part, at in enumerate(blocks):
        grad_queries[at, :] = cotangent[at, :] * convolved(0, part)
    copies[0].start()
    for part, at in enumerate(blocks):
        grad_filter[at, :] = convolved(2, part)
    copies[3].start()
    for copy in copies:
        copy.wait()


def call(kernel, devices, out_shape, scratch=(), **specs):
    def bound(*refs):
        kernel(devices, *refs)

    return pl.pallas_call(
        bound,
        out_shape=out_shape,
        scratch_shapes=scratch,
        compiler_params=pltpu.CompilerParams(vmem_limit_bytes=VMEM_LIMIT),
        **specs,
    )


def local(queries, keys, values, cotangent, filt, skip):
    segment, channels = queries.shape
    devices = lax.axis_size(AXES)
    tokens = segment * devices
    rows = tokens // LANES
    share = channels // devices
    block = 3 * (segment // LANES) * share
    flat = pltpu.VMEM((devices * block, LANES), jnp.float32)

    def exchange(array):
        array = array.reshape(devices, block, LANES)
        array = lax.all_to_all(array, EXCHANGE, split_axis=0, concat_axis=0, tiled=True)
        return array.reshape(devices * block, LANES)

    whole = pltpu.VMEM((segment, channels), jnp.float32)
    result = jax.ShapeDtypeStruct(whole.shape, whole.dtype)
    far = pl.BlockSpec(memory_space=pltpu.HBM)
    near = pl.BlockSpec(memory_space=pltpu.VMEM)
    operands = (skip.reshape(1, channels), filt, keys, values, cotangent, queries)
    operands = tuple(pltpu.with_memory_space_constraint(array, pltpu.HBM) for array in operands)
    scratch = (pltpu.VMEM((1, channels), jnp.float32),) + (whole,) * 5 + (pltpu.SemaphoreType.DMA((6,)),)
    gate = call(gate_kernel, devices, flat, scratch, in_specs=(far,) * 6)
    arrived = exchange(gate(*operands))
    wide = pltpu.VMEM((3 * share * rows, 2 * LANES), jnp.bfloat16)
    constants = tuple(jnp.asarray(table) for table in tables(tokens, devices, lax.axis_size(AXES[0])))
    convolved = call(conv_kernel, devices, flat, (wide, wide))(arrived, *constants)
    returned = exchange(convolved)
    finish = call(
        finish_kernel,
        devices,
        (result,) * 4,
        (whole,) * 4 + (pltpu.SemaphoreType.DMA((4,)),),
        in_specs=(near,) * 4,
        out_specs=(far,) * 4,
    )
    return tuple(finish(returned, keys, values, cotangent))


def solution(mesh):
    whole = P(AXES, None)
    return jax.shard_map(
        local,
        mesh=mesh,
        in_specs=(whole,) * 5 + (P(),),
        out_specs=(whole,) * 4,
        check_vma=False,
    )
```

```python
import math

import jax
import jax.numpy as jnp
import ml_dtypes
import numpy as np
from jax import lax
from jax.experimental import pallas as pl
from jax.experimental.pallas import tpu as pltpu
from jax.sharding import PartitionSpec as P

LANES = 128
AXES = ("sa", "sb")
VMEM_LIMIT = 48 * 1024 * 1024


def halves(matrix):
    high = matrix.astype(ml_dtypes.bfloat16)
    low = (matrix - high.astype(np.float64)).astype(ml_dtypes.bfloat16)
    return high, low


def exchange_order(planes, width):
    return [plane * width + place for place in range(width) for plane in reversed(range(planes))]


def tables(tokens, devices, group):
    rows = tokens // LANES
    parts = rows // devices
    order = (np.array(group)[None, :] * parts + np.arange(parts)[:, None]).reshape(-1)
    half_step = np.arange(rows) + 0.5
    lane = np.arange(LANES)
    angle = 2.0 * np.pi / (2 * rows) * half_step[:, None] * order[None, :]
    first = np.concatenate([np.cos(angle), -np.sin(angle)], axis=0)
    turn_angle = 2.0 * np.pi / (2 * tokens) * half_step[:, None] * lane[None, :]
    turn = np.stack([np.cos(turn_angle), -np.sin(turn_angle)]).astype(np.float32)
    lane_angle = 2.0 * np.pi / LANES * ((lane[:, None] * lane[None, :]) % LANES)
    cosine, sine = np.cos(lane_angle), np.sin(lane_angle)
    second = np.block([[cosine, -sine], [sine, cosine]])
    factor = 1.0 / (tokens * math.sqrt(tokens))
    last = np.concatenate([np.cos(angle).T, np.sin(angle).T], axis=1) * factor
    first_high, first_low = halves(first)
    last_high, last_low = halves(last)
    second_high, second_low = halves(second)
    return (
        np.concatenate([first_high, first_high, first_low], axis=1),
        turn,
        np.stack([second_high, second_low]),
        np.concatenate([last_high, last_high, last_low], axis=1),
    )


def split(array):
    high = array.astype(jnp.bfloat16)
    low = (array - high.astype(jnp.float32)).astype(jnp.bfloat16)
    return high, low


def stacked(array):
    high, low = split(array)
    return jnp.concatenate([high, low, high], axis=0)


def matmul(left, right):
    return jnp.dot(left, right, preferred_element_type=jnp.float32)


def gate_kernel(devices, *refs):
    far = refs[:6]
    out = refs[6]
    near = refs[7:13]
    arrivals = refs[13]
    copies = [
        pltpu.make_async_copy(source, target, arrivals.at[number])
        for number, (source, target) in enumerate(zip(far, near))
    ]
    for copy in copies:
        copy.start()
    skip, filt, keys, values, cotangent, queries = near
    segment, channels = queries.shape
    parts = segment // LANES
    share = channels // devices
    block = 3 * parts * share
    for number in (1, 0, 2):
        needed = {0: (2, 3), 1: (0, 1), 2: (4, 5)}[number]
        for index in needed:
            copies[index].wait()
        if number == 1:
            first_tap = jnp.where(lax.axis_index(AXES) == 0, math.sqrt(devices * segment), 0.0)
            filt[0:1, :] += first_tap * skip[...]
        for part in range(parts):
            at = pl.ds(part * LANES, LANES)
            if number == 0:
                signal = keys[at, :] * values[at, :]
            elif number == 1:
                signal = filt[at, :]
            else:
                signal = cotangent[at, :] * queries[at, :]
            turned = signal.T
            for channel in range(share):
                row = (number * parts + part) * share + channel
                out[pl.ds(row, devices, stride=block), :] = turned[
                    channel * devices : (channel + 1) * devices, :
                ]


def conv_kernel(devices, arrived, first, turn, second, last, out, high, low):
    rows = turn.shape[1]
    parts = rows // devices
    block = arrived.shape[0] // devices
    share = block // (3 * parts)
    turn_real = turn[0]
    turn_imag = turn[1]

    def gathered(number, channel):
        pieces = []
        for part in range(parts):
            row = (number * parts + part) * share + channel
            pieces.append(arrived[pl.ds(row, devices, stride=block), :])
        return jnp.concatenate(pieces, axis=0)

    def hold(number, channel, real, imag):
        at = pl.ds((channel * 3 + number) * rows, rows)
        for value, lanes in ((real, pl.ds(0, LANES)), (imag, pl.ds(LANES, LANES))):
            high[at, lanes], low[at, lanes] = split(value)

    def lanes_transform(channel):
        at = pl.ds(channel * 3 * rows, 3 * rows)
        result = (
            matmul(high[at, :], second[0])
            + matmul(high[at, :], second[1])
            + matmul(low[at, :], second[0])
        )
        pieces = []
        for number in range(3):
            piece = result[number * rows : (number + 1) * rows]
            pieces.append((piece[:, 0:LANES], piece[:, LANES : 2 * LANES]))
        return pieces

    for number in range(3):
        signals = [stacked(gathered(number, channel)) for channel in range(share)]
        spread = matmul(first[...], jnp.concatenate(signals, axis=1))
        for channel in range(share):
            lanes = slice(channel * LANES, (channel + 1) * LANES)
            real = spread[:rows, lanes]
            imag = spread[rows:, lanes]
            hold(
                number,
                channel,
                real * turn_real - imag * turn_imag,
                real * turn_imag + imag * turn_real,
            )
    for channel in range(share):
        (gr, gi), (fr, fi), (ur, ui) = lanes_transform(channel)
        hold(0, channel, fr * gr - fi * gi, -(fr * gi + fi * gr))
        hold(1, channel, fr * ur + fi * ui, fi * ur - fr * ui)
        hold(2, channel, gr * ur + gi * ui, gi * ur - gr * ui)
    turned = [[], [], []]
    for channel in range(share):
        for number, (real, imag) in enumerate(lanes_transform(channel)):
            both = (real * turn_real - imag * turn_imag, real * turn_imag + imag * turn_real)
            turned[number].append(stacked(jnp.concatenate(both, axis=0)))
    for number in range(3):
        result = matmul(last[...], jnp.concatenate(turned[number], axis=1))
        for channel in range(share):
            lanes = slice(channel * LANES, (channel + 1) * LANES)
            for part in range(parts):
                row = (number * parts + part) * share + channel
                out[pl.ds(row, devices, stride=block), :] = result[
                    part * devices : (part + 1) * devices, lanes
                ]


def finish_kernel(devices, arrived, keys, values, cotangent, *refs):
    far = refs[:4]
    near = refs[4:8]
    departures = refs[8]
    grad_queries, grad_keys, grad_values, grad_filter = near
    segment, channels = keys.shape
    parts = segment // LANES
    share = channels // devices
    block = 3 * parts * share
    copies = [
        pltpu.make_async_copy(source, target, departures.at[number])
        for number, (source, target) in enumerate(zip(near, far))
    ]

    def convolved(number, part):
        pieces = []
        for channel in range(share):
            row = (number * parts + part) * share + channel
            pieces.append(arrived[pl.ds(row, devices, stride=block), :])
        return jnp.concatenate(pieces, axis=0).T

    blocks = [pl.ds(part * LANES, LANES) for part in range(parts)]
    for part, at in enumerate(blocks):
        back_signal = convolved(1, part)
        grad_keys[at, :] = back_signal * values[at, :]
        grad_values[at, :] = back_signal * keys[at, :]
    copies[1].start()
    copies[2].start()
    for part, at in enumerate(blocks):
        grad_queries[at, :] = cotangent[at, :] * convolved(0, part)
    copies[0].start()
    for part, at in enumerate(blocks):
        grad_filter[at, :] = convolved(2, part)
    copies[3].start()
    for copy in copies:
        copy.wait()


def call(kernel, devices, out_shape, scratch=(), **specs):
    def bound(*refs):
        kernel(devices, *refs)

    return pl.pallas_call(
        bound,
        out_shape=out_shape,
        scratch_shapes=scratch,
        compiler_params=pltpu.CompilerParams(vmem_limit_bytes=VMEM_LIMIT),
        **specs,
    )


def local(queries, keys, values, cotangent, filt, skip):
    segment, channels = queries.shape
    devices = lax.axis_size(AXES)
    tokens = segment * devices
    rows = tokens // LANES
    share = channels // devices
    block = 3 * (segment // LANES) * share
    flat = pltpu.VMEM((devices * block, LANES), jnp.float32)

    group = exchange_order(lax.axis_size(AXES[0]), lax.axis_size(AXES[1]))

    def exchange(array):
        array = lax.all_to_all(
            array, AXES, split_axis=0, concat_axis=0, axis_index_groups=[group], tiled=True
        )
        return array.reshape(devices * block, LANES)

    whole = pltpu.VMEM((segment, channels), jnp.float32)
    result = jax.ShapeDtypeStruct(whole.shape, whole.dtype)
    far = pl.BlockSpec(memory_space=pltpu.HBM)
    near = pl.BlockSpec(memory_space=pltpu.VMEM)
    operands = (skip.reshape(1, channels), filt, keys, values, cotangent, queries)
    operands = tuple(pltpu.with_memory_space_constraint(array, pltpu.HBM) for array in operands)
    scratch = (pltpu.VMEM((1, channels), jnp.float32),) + (whole,) * 5 + (pltpu.SemaphoreType.DMA((6,)),)
    gate = call(gate_kernel, devices, flat, scratch, in_specs=(far,) * 6)
    arrived = exchange(gate(*operands))
    wide = pltpu.VMEM((3 * share * rows, 2 * LANES), jnp.bfloat16)
    constants = tuple(jnp.asarray(table) for table in tables(tokens, devices, group))
    convolved = call(conv_kernel, devices, flat, (wide, wide))(arrived, *constants)
    returned = exchange(convolved)
    finish = call(
        finish_kernel,
        devices,
        (result,) * 4,
        (whole,) * 4 + (pltpu.SemaphoreType.DMA((4,)),),
        in_specs=(near,) * 4,
        out_specs=(far,) * 4,
    )
    return tuple(finish(returned, keys, values, cotangent))


def solution(mesh):
    whole = P(AXES, None)
    return jax.shard_map(
        local,
        mesh=mesh,
        in_specs=(whole,) * 5 + (P(),),
        out_specs=(whole,) * 4,
        check_vma=False,
    )
```

```python
import math

import jax
import jax.numpy as jnp
import ml_dtypes
import numpy as np
from jax import lax
from jax.experimental import pallas as pl
from jax.experimental.pallas import tpu as pltpu
from jax.sharding import PartitionSpec as P

LANES = 128
AXES = ("sa", "sb")
VMEM_LIMIT = 48 * 1024 * 1024


def halves(matrix):
    high = matrix.astype(ml_dtypes.bfloat16)
    low = (matrix - high.astype(np.float64)).astype(ml_dtypes.bfloat16)
    return high, low


def exchange_order(planes, width):
    lower = planes // 2
    turns = [plane for pair in zip(range(lower), range(lower, planes)) for plane in pair]
    return [plane * width + place for place in range(width) for plane in reversed(turns)]


def tables(tokens, devices, group):
    rows = tokens // LANES
    parts = rows // devices
    order = (np.array(group)[None, :] * parts + np.arange(parts)[:, None]).reshape(-1)
    half_step = np.arange(rows) + 0.5
    lane = np.arange(LANES)
    angle = 2.0 * np.pi / (2 * rows) * half_step[:, None] * order[None, :]
    first = np.concatenate([np.cos(angle), -np.sin(angle)], axis=0)
    turn_angle = 2.0 * np.pi / (2 * tokens) * half_step[:, None] * lane[None, :]
    turn = np.stack([np.cos(turn_angle), -np.sin(turn_angle)]).astype(np.float32)
    lane_angle = 2.0 * np.pi / LANES * ((lane[:, None] * lane[None, :]) % LANES)
    cosine, sine = np.cos(lane_angle), np.sin(lane_angle)
    second = np.block([[cosine, -sine], [sine, cosine]])
    factor = 1.0 / (tokens * math.sqrt(tokens))
    last = np.concatenate([np.cos(angle).T, np.sin(angle).T], axis=1) * factor
    first_high, first_low = halves(first)
    last_high, last_low = halves(last)
    second_high, second_low = halves(second)
    return (
        np.concatenate([first_high, first_high, first_low], axis=1),
        turn,
        np.stack([second_high, second_low]),
        np.concatenate([last_high, last_high, last_low], axis=1),
    )


def split(array):
    high = array.astype(jnp.bfloat16)
    low = (array - high.astype(jnp.float32)).astype(jnp.bfloat16)
    return high, low


def stacked(array):
    high, low = split(array)
    return jnp.concatenate([high, low, high], axis=0)


def matmul(left, right):
    return jnp.dot(left, right, preferred_element_type=jnp.float32)


def gate_kernel(devices, *refs):
    far = refs[:6]
    out = refs[6]
    near = refs[7:13]
    arrivals = refs[13]
    copies = [
        pltpu.make_async_copy(source, target, arrivals.at[number])
        for number, (source, target) in enumerate(zip(far, near))
    ]
    for copy in copies:
        copy.start()
    skip, filt, keys, values, cotangent, queries = near
    segment, channels = queries.shape
    parts = segment // LANES
    share = channels // devices
    block = 3 * parts * share
    for number in (1, 0, 2):
        needed = {0: (2, 3), 1: (0, 1), 2: (4, 5)}[number]
        for index in needed:
            copies[index].wait()
        if number == 1:
            first_tap = jnp.where(lax.axis_index(AXES) == 0, math.sqrt(devices * segment), 0.0)
            filt[0:1, :] += first_tap * skip[...]
        for part in range(parts):
            at = pl.ds(part * LANES, LANES)
            if number == 0:
                signal = keys[at, :] * values[at, :]
            elif number == 1:
                signal = filt[at, :]
            else:
                signal = cotangent[at, :] * queries[at, :]
            turned = signal.T
            for channel in range(share):
                row = (number * parts + part) * share + channel
                out[pl.ds(row, devices, stride=block), :] = turned[
                    channel * devices : (channel + 1) * devices, :
                ]


def conv_kernel(devices, arrived, first, turn, second, last, out, high, low):
    rows = turn.shape[1]
    parts = rows // devices
    block = arrived.shape[0] // devices
    share = block // (3 * parts)
    turn_real = turn[0]
    turn_imag = turn[1]

    def gathered(number, channel):
        pieces = []
        for part in range(parts):
            row = (number * parts + part) * share + channel
            pieces.append(arrived[pl.ds(row, devices, stride=block), :])
        return jnp.concatenate(pieces, axis=0)

    def hold(number, channel, real, imag):
        at = pl.ds((channel * 3 + number) * rows, rows)
        for value, lanes in ((real, pl.ds(0, LANES)), (imag, pl.ds(LANES, LANES))):
            high[at, lanes], low[at, lanes] = split(value)

    def lanes_transform(channel):
        at = pl.ds(channel * 3 * rows, 3 * rows)
        result = (
            matmul(high[at, :], second[0])
            + matmul(high[at, :], second[1])
            + matmul(low[at, :], second[0])
        )
        pieces = []
        for number in range(3):
            piece = result[number * rows : (number + 1) * rows]
            pieces.append((piece[:, 0:LANES], piece[:, LANES : 2 * LANES]))
        return pieces

    for number in range(3):
        signals = [stacked(gathered(number, channel)) for channel in range(share)]
        spread = matmul(first[...], jnp.concatenate(signals, axis=1))
        for channel in range(share):
            lanes = slice(channel * LANES, (channel + 1) * LANES)
            real = spread[:rows, lanes]
            imag = spread[rows:, lanes]
            hold(
                number,
                channel,
                real * turn_real - imag * turn_imag,
                real * turn_imag + imag * turn_real,
            )
    for channel in range(share):
        (gr, gi), (fr, fi), (ur, ui) = lanes_transform(channel)
        hold(0, channel, fr * gr - fi * gi, -(fr * gi + fi * gr))
        hold(1, channel, fr * ur + fi * ui, fi * ur - fr * ui)
        hold(2, channel, gr * ur + gi * ui, gi * ur - gr * ui)
    turned = [[], [], []]
    for channel in range(share):
        for number, (real, imag) in enumerate(lanes_transform(channel)):
            both = (real * turn_real - imag * turn_imag, real * turn_imag + imag * turn_real)
            turned[number].append(stacked(jnp.concatenate(both, axis=0)))
    for number in range(3):
        result = matmul(last[...], jnp.concatenate(turned[number], axis=1))
        for channel in range(share):
            lanes = slice(channel * LANES, (channel + 1) * LANES)
            for part in range(parts):
                row = (number * parts + part) * share + channel
                out[pl.ds(row, devices, stride=block), :] = result[
                    part * devices : (part + 1) * devices, lanes
                ]


def finish_kernel(devices, arrived, keys, values, cotangent, *refs):
    far = refs[:4]
    near = refs[4:8]
    departures = refs[8]
    grad_queries, grad_keys, grad_values, grad_filter = near
    segment, channels = keys.shape
    parts = segment // LANES
    share = channels // devices
    block = 3 * parts * share
    copies = [
        pltpu.make_async_copy(source, target, departures.at[number])
        for number, (source, target) in enumerate(zip(near, far))
    ]

    def convolved(number, part):
        pieces = []
        for channel in range(share):
            row = (number * parts + part) * share + channel
            pieces.append(arrived[pl.ds(row, devices, stride=block), :])
        return jnp.concatenate(pieces, axis=0).T

    blocks = [pl.ds(part * LANES, LANES) for part in range(parts)]
    for part, at in enumerate(blocks):
        back_signal = convolved(1, part)
        grad_keys[at, :] = back_signal * values[at, :]
        grad_values[at, :] = back_signal * keys[at, :]
    copies[1].start()
    copies[2].start()
    for part, at in enumerate(blocks):
        grad_queries[at, :] = cotangent[at, :] * convolved(0, part)
    copies[0].start()
    for part, at in enumerate(blocks):
        grad_filter[at, :] = convolved(2, part)
    copies[3].start()
    for copy in copies:
        copy.wait()


def call(kernel, devices, out_shape, scratch=(), **specs):
    def bound(*refs):
        kernel(devices, *refs)

    return pl.pallas_call(
        bound,
        out_shape=out_shape,
        scratch_shapes=scratch,
        compiler_params=pltpu.CompilerParams(vmem_limit_bytes=VMEM_LIMIT),
        **specs,
    )


def local(queries, keys, values, cotangent, filt, skip):
    segment, channels = queries.shape
    devices = lax.axis_size(AXES)
    tokens = segment * devices
    rows = tokens // LANES
    share = channels // devices
    block = 3 * (segment // LANES) * share
    flat = pltpu.VMEM((devices * block, LANES), jnp.float32)

    group = exchange_order(lax.axis_size(AXES[0]), lax.axis_size(AXES[1]))

    def exchange(array):
        array = lax.all_to_all(
            array, AXES, split_axis=0, concat_axis=0, axis_index_groups=[group], tiled=True
        )
        return array.reshape(devices * block, LANES)

    whole = pltpu.VMEM((segment, channels), jnp.float32)
    result = jax.ShapeDtypeStruct(whole.shape, whole.dtype)
    far = pl.BlockSpec(memory_space=pltpu.HBM)
    near = pl.BlockSpec(memory_space=pltpu.VMEM)
    operands = (skip.reshape(1, channels), filt, keys, values, cotangent, queries)
    operands = tuple(pltpu.with_memory_space_constraint(array, pltpu.HBM) for array in operands)
    scratch = (pltpu.VMEM((1, channels), jnp.float32),) + (whole,) * 5 + (pltpu.SemaphoreType.DMA((6,)),)
    gate = call(gate_kernel, devices, flat, scratch, in_specs=(far,) * 6)
    arrived = exchange(gate(*operands))
    wide = pltpu.VMEM((3 * share * rows, 2 * LANES), jnp.bfloat16)
    constants = tuple(jnp.asarray(table) for table in tables(tokens, devices, group))
    convolved = call(conv_kernel, devices, flat, (wide, wide))(arrived, *constants)
    returned = exchange(convolved)
    finish = call(
        finish_kernel,
        devices,
        (result,) * 4,
        (whole,) * 4 + (pltpu.SemaphoreType.DMA((4,)),),
        in_specs=(near,) * 4,
        out_specs=(far,) * 4,
    )
    return tuple(finish(returned, keys, values, cotangent))


def solution(mesh):
    whole = P(AXES, None)
    return jax.shard_map(
        local,
        mesh=mesh,
        in_specs=(whole,) * 5 + (P(),),
        out_specs=(whole,) * 4,
        check_vma=False,
    )
```

```python
import math

import jax
import jax.numpy as jnp
import ml_dtypes
import numpy as np
from jax import lax
from jax.experimental import pallas as pl
from jax.experimental.pallas import tpu as pltpu
from jax.sharding import PartitionSpec as P

LANES = 128
AXES = ("sa", "sb")
VMEM_LIMIT = 48 * 1024 * 1024


def halves(matrix):
    high = matrix.astype(ml_dtypes.bfloat16)
    low = (matrix - high.astype(np.float64)).astype(ml_dtypes.bfloat16)
    return high, low


def exchange_order(planes, width):
    return [-plane % planes * width + place for place in range(width) for plane in range(planes)]


def tables(tokens, devices, group):
    rows = tokens // LANES
    parts = rows // devices
    order = (np.array(group)[None, :] * parts + np.arange(parts)[:, None]).reshape(-1)
    half_step = np.arange(rows) + 0.5
    lane = np.arange(LANES)
    angle = 2.0 * np.pi / (2 * rows) * half_step[:, None] * order[None, :]
    first = np.concatenate([np.cos(angle), -np.sin(angle)], axis=0)
    turn_angle = 2.0 * np.pi / (2 * tokens) * half_step[:, None] * lane[None, :]
    turn = np.stack([np.cos(turn_angle), -np.sin(turn_angle)]).astype(np.float32)
    lane_angle = 2.0 * np.pi / LANES * ((lane[:, None] * lane[None, :]) % LANES)
    cosine, sine = np.cos(lane_angle), np.sin(lane_angle)
    second = np.block([[cosine, -sine], [sine, cosine]])
    factor = 1.0 / (tokens * math.sqrt(tokens))
    last = np.concatenate([np.cos(angle).T, np.sin(angle).T], axis=1) * factor
    first_high, first_low = halves(first)
    last_high, last_low = halves(last)
    second_high, second_low = halves(second)
    return (
        np.concatenate([first_high, first_high, first_low], axis=1),
        turn,
        np.stack([second_high, second_low]),
        np.concatenate([last_high, last_high, last_low], axis=1),
    )


def split(array):
    high = array.astype(jnp.bfloat16)
    low = (array - high.astype(jnp.float32)).astype(jnp.bfloat16)
    return high, low


def stacked(array):
    high, low = split(array)
    return jnp.concatenate([high, low, high], axis=0)


def matmul(left, right):
    return jnp.dot(left, right, preferred_element_type=jnp.float32)


def gate_kernel(devices, *refs):
    far = refs[:6]
    out = refs[6]
    near = refs[7:13]
    arrivals = refs[13]
    copies = [
        pltpu.make_async_copy(source, target, arrivals.at[number])
        for number, (source, target) in enumerate(zip(far, near))
    ]
    for copy in copies:
        copy.start()
    skip, filt, keys, values, cotangent, queries = near
    segment, channels = queries.shape
    parts = segment // LANES
    share = channels // devices
    block = 3 * parts * share
    for number in (1, 0, 2):
        needed = {0: (2, 3), 1: (0, 1), 2: (4, 5)}[number]
        for index in needed:
            copies[index].wait()
        if number == 1:
            first_tap = jnp.where(lax.axis_index(AXES) == 0, math.sqrt(devices * segment), 0.0)
            filt[0:1, :] += first_tap * skip[...]
        for part in range(parts):
            at = pl.ds(part * LANES, LANES)
            if number == 0:
                signal = keys[at, :] * values[at, :]
            elif number == 1:
                signal = filt[at, :]
            else:
                signal = cotangent[at, :] * queries[at, :]
            turned = signal.T
            for channel in range(share):
                row = (number * parts + part) * share + channel
                out[pl.ds(row, devices, stride=block), :] = turned[
                    channel * devices : (channel + 1) * devices, :
                ]


def conv_kernel(devices, arrived, first, turn, second, last, out, high, low):
    rows = turn.shape[1]
    parts = rows // devices
    block = arrived.shape[0] // devices
    share = block // (3 * parts)
    turn_real = turn[0]
    turn_imag = turn[1]

    def gathered(number, channel):
        pieces = []
        for part in range(parts):
            row = (number * parts + part) * share + channel
            pieces.append(arrived[pl.ds(row, devices, stride=block), :])
        return jnp.concatenate(pieces, axis=0)

    def hold(number, channel, real, imag):
        at = pl.ds((channel * 3 + number) * rows, rows)
        for value, lanes in ((real, pl.ds(0, LANES)), (imag, pl.ds(LANES, LANES))):
            high[at, lanes], low[at, lanes] = split(value)

    def lanes_transform(channel):
        at = pl.ds(channel * 3 * rows, 3 * rows)
        result = (
            matmul(high[at, :], second[0])
            + matmul(high[at, :], second[1])
            + matmul(low[at, :], second[0])
        )
        pieces = []
        for number in range(3):
            piece = result[number * rows : (number + 1) * rows]
            pieces.append((piece[:, 0:LANES], piece[:, LANES : 2 * LANES]))
        return pieces

    for number in range(3):
        signals = [stacked(gathered(number, channel)) for channel in range(share)]
        spread = matmul(first[...], jnp.concatenate(signals, axis=1))
        for channel in range(share):
            lanes = slice(channel * LANES, (channel + 1) * LANES)
            real = spread[:rows, lanes]
            imag = spread[rows:, lanes]
            hold(
                number,
                channel,
                real * turn_real - imag * turn_imag,
                real * turn_imag + imag * turn_real,
            )
    for channel in range(share):
        (gr, gi), (fr, fi), (ur, ui) = lanes_transform(channel)
        hold(0, channel, fr * gr - fi * gi, -(fr * gi + fi * gr))
        hold(1, channel, fr * ur + fi * ui, fi * ur - fr * ui)
        hold(2, channel, gr * ur + gi * ui, gi * ur - gr * ui)
    turned = [[], [], []]
    for channel in range(share):
        for number, (real, imag) in enumerate(lanes_transform(channel)):
            both = (real * turn_real - imag * turn_imag, real * turn_imag + imag * turn_real)
            turned[number].append(stacked(jnp.concatenate(both, axis=0)))
    for number in range(3):
        result = matmul(last[...], jnp.concatenate(turned[number], axis=1))
        for channel in range(share):
            lanes = slice(channel * LANES, (channel + 1) * LANES)
            for part in range(parts):
                row = (number * parts + part) * share + channel
                out[pl.ds(row, devices, stride=block), :] = result[
                    part * devices : (part + 1) * devices, lanes
                ]


def finish_kernel(devices, arrived, keys, values, cotangent, *refs):
    far = refs[:4]
    near = refs[4:8]
    departures = refs[8]
    grad_queries, grad_keys, grad_values, grad_filter = near
    segment, channels = keys.shape
    parts = segment // LANES
    share = channels // devices
    block = 3 * parts * share
    copies = [
        pltpu.make_async_copy(source, target, departures.at[number])
        for number, (source, target) in enumerate(zip(near, far))
    ]

    def convolved(number, part):
        pieces = []
        for channel in range(share):
            row = (number * parts + part) * share + channel
            pieces.append(arrived[pl.ds(row, devices, stride=block), :])
        return jnp.concatenate(pieces, axis=0).T

    blocks = [pl.ds(part * LANES, LANES) for part in range(parts)]
    for part, at in enumerate(blocks):
        back_signal = convolved(1, part)
        grad_keys[at, :] = back_signal * values[at, :]
        grad_values[at, :] = back_signal * keys[at, :]
    copies[1].start()
    copies[2].start()
    for part, at in enumerate(blocks):
        grad_queries[at, :] = cotangent[at, :] * convolved(0, part)
    copies[0].start()
    for part, at in enumerate(blocks):
        grad_filter[at, :] = convolved(2, part)
    copies[3].start()
    for copy in copies:
        copy.wait()


def call(kernel, devices, out_shape, scratch=(), **specs):
    def bound(*refs):
        kernel(devices, *refs)

    return pl.pallas_call(
        bound,
        out_shape=out_shape,
        scratch_shapes=scratch,
        compiler_params=pltpu.CompilerParams(vmem_limit_bytes=VMEM_LIMIT),
        **specs,
    )


def local(queries, keys, values, cotangent, filt, skip):
    segment, channels = queries.shape
    devices = lax.axis_size(AXES)
    tokens = segment * devices
    rows = tokens // LANES
    share = channels // devices
    block = 3 * (segment // LANES) * share
    flat = pltpu.VMEM((devices * block, LANES), jnp.float32)

    group = exchange_order(lax.axis_size(AXES[0]), lax.axis_size(AXES[1]))

    def exchange(array):
        array = lax.all_to_all(
            array, AXES, split_axis=0, concat_axis=0, axis_index_groups=[group], tiled=True
        )
        return array.reshape(devices * block, LANES)

    whole = pltpu.VMEM((segment, channels), jnp.float32)
    result = jax.ShapeDtypeStruct(whole.shape, whole.dtype)
    far = pl.BlockSpec(memory_space=pltpu.HBM)
    near = pl.BlockSpec(memory_space=pltpu.VMEM)
    operands = (skip.reshape(1, channels), filt, keys, values, cotangent, queries)
    operands = tuple(pltpu.with_memory_space_constraint(array, pltpu.HBM) for array in operands)
    scratch = (pltpu.VMEM((1, channels), jnp.float32),) + (whole,) * 5 + (pltpu.SemaphoreType.DMA((6,)),)
    gate = call(gate_kernel, devices, flat, scratch, in_specs=(far,) * 6)
    arrived = exchange(gate(*operands))
    wide = pltpu.VMEM((3 * share * rows, 2 * LANES), jnp.bfloat16)
    constants = tuple(jnp.asarray(table) for table in tables(tokens, devices, group))
    convolved = call(conv_kernel, devices, flat, (wide, wide))(arrived, *constants)
    returned = exchange(convolved)
    finish = call(
        finish_kernel,
        devices,
        (result,) * 4,
        (whole,) * 4 + (pltpu.SemaphoreType.DMA((4,)),),
        in_specs=(near,) * 4,
        out_specs=(far,) * 4,
    )
    return tuple(finish(returned, keys, values, cotangent))


def solution(mesh):
    whole = P(AXES, None)
    return jax.shard_map(
        local,
        mesh=mesh,
        in_specs=(whole,) * 5 + (P(),),
        out_specs=(whole,) * 4,
        check_vma=False,
    )
```

```python
import math

import jax
import jax.numpy as jnp
import ml_dtypes
import numpy as np
from jax import lax
from jax.experimental import pallas as pl
from jax.experimental.pallas import tpu as pltpu
from jax.sharding import PartitionSpec as P

LANES = 128
AXES = ("sa", "sb")
VMEM_LIMIT = 48 * 1024 * 1024


def halves(matrix):
    high = matrix.astype(ml_dtypes.bfloat16)
    low = (matrix - high.astype(np.float64)).astype(ml_dtypes.bfloat16)
    return high, low


def exchange_order(planes, width):
    return [(1 - plane) % planes * width + place for place in range(width) for plane in range(planes)]


def tables(tokens, devices, group):
    rows = tokens // LANES
    parts = rows // devices
    order = (np.array(group)[None, :] * parts + np.arange(parts)[:, None]).reshape(-1)
    half_step = np.arange(rows) + 0.5
    lane = np.arange(LANES)
    angle = 2.0 * np.pi / (2 * rows) * half_step[:, None] * order[None, :]
    first = np.concatenate([np.cos(angle), -np.sin(angle)], axis=0)
    turn_angle = 2.0 * np.pi / (2 * tokens) * half_step[:, None] * lane[None, :]
    turn = np.stack([np.cos(turn_angle), -np.sin(turn_angle)]).astype(np.float32)
    lane_angle = 2.0 * np.pi / LANES * ((lane[:, None] * lane[None, :]) % LANES)
    cosine, sine = np.cos(lane_angle), np.sin(lane_angle)
    second = np.block([[cosine, -sine], [sine, cosine]])
    factor = 1.0 / (tokens * math.sqrt(tokens))
    last = np.concatenate([np.cos(angle).T, np.sin(angle).T], axis=1) * factor
    first_high, first_low = halves(first)
    last_high, last_low = halves(last)
    second_high, second_low = halves(second)
    return (
        np.concatenate([first_high, first_high, first_low], axis=1),
        turn,
        np.stack([second_high, second_low]),
        np.concatenate([last_high, last_high, last_low], axis=1),
    )


def split(array):
    high = array.astype(jnp.bfloat16)
    low = (array - high.astype(jnp.float32)).astype(jnp.bfloat16)
    return high, low


def stacked(array):
    high, low = split(array)
    return jnp.concatenate([high, low, high], axis=0)


def matmul(left, right):
    return jnp.dot(left, right, preferred_element_type=jnp.float32)


def gate_kernel(devices, *refs):
    far = refs[:6]
    out = refs[6]
    near = refs[7:13]
    arrivals = refs[13]
    copies = [
        pltpu.make_async_copy(source, target, arrivals.at[number])
        for number, (source, target) in enumerate(zip(far, near))
    ]
    for copy in copies:
        copy.start()
    skip, filt, keys, values, cotangent, queries = near
    segment, channels = queries.shape
    parts = segment // LANES
    share = channels // devices
    block = 3 * parts * share
    for number in (1, 0, 2):
        needed = {0: (2, 3), 1: (0, 1), 2: (4, 5)}[number]
        for index in needed:
            copies[index].wait()
        if number == 1:
            first_tap = jnp.where(lax.axis_index(AXES) == 0, math.sqrt(devices * segment), 0.0)
            filt[0:1, :] += first_tap * skip[...]
        for part in range(parts):
            at = pl.ds(part * LANES, LANES)
            if number == 0:
                signal = keys[at, :] * values[at, :]
            elif number == 1:
                signal = filt[at, :]
            else:
                signal = cotangent[at, :] * queries[at, :]
            turned = signal.T
            for channel in range(share):
                row = (number * parts + part) * share + channel
                out[pl.ds(row, devices, stride=block), :] = turned[
                    channel * devices : (channel + 1) * devices, :
                ]


def conv_kernel(devices, arrived, first, turn, second, last, out, high, low):
    rows = turn.shape[1]
    parts = rows // devices
    block = arrived.shape[0] // devices
    share = block // (3 * parts)
    turn_real = turn[0]
    turn_imag = turn[1]

    def gathered(number, channel):
        pieces = []
        for part in range(parts):
            row = (number * parts + part) * share + channel
            pieces.append(arrived[pl.ds(row, devices, stride=block), :])
        return jnp.concatenate(pieces, axis=0)

    def hold(number, channel, real, imag):
        at = pl.ds((channel * 3 + number) * rows, rows)
        for value, lanes in ((real, pl.ds(0, LANES)), (imag, pl.ds(LANES, LANES))):
            high[at, lanes], low[at, lanes] = split(value)

    def lanes_transform(channel):
        at = pl.ds(channel * 3 * rows, 3 * rows)
        result = (
            matmul(high[at, :], second[0])
            + matmul(high[at, :], second[1])
            + matmul(low[at, :], second[0])
        )
        pieces = []
        for number in range(3):
            piece = result[number * rows : (number + 1) * rows]
            pieces.append((piece[:, 0:LANES], piece[:, LANES : 2 * LANES]))
        return pieces

    for number in range(3):
        signals = [stacked(gathered(number, channel)) for channel in range(share)]
        spread = matmul(first[...], jnp.concatenate(signals, axis=1))
        for channel in range(share):
            lanes = slice(channel * LANES, (channel + 1) * LANES)
            real = spread[:rows, lanes]
            imag = spread[rows:, lanes]
            hold(
                number,
                channel,
                real * turn_real - imag * turn_imag,
                real * turn_imag + imag * turn_real,
            )
    for channel in range(share):
        (gr, gi), (fr, fi), (ur, ui) = lanes_transform(channel)
        hold(0, channel, fr * gr - fi * gi, -(fr * gi + fi * gr))
        hold(1, channel, fr * ur + fi * ui, fi * ur - fr * ui)
        hold(2, channel, gr * ur + gi * ui, gi * ur - gr * ui)
    turned = [[], [], []]
    for channel in range(share):
        for number, (real, imag) in enumerate(lanes_transform(channel)):
            both = (real * turn_real - imag * turn_imag, real * turn_imag + imag * turn_real)
            turned[number].append(stacked(jnp.concatenate(both, axis=0)))
    for number in range(3):
        result = matmul(last[...], jnp.concatenate(turned[number], axis=1))
        for channel in range(share):
            lanes = slice(channel * LANES, (channel + 1) * LANES)
            for part in range(parts):
                row = (number * parts + part) * share + channel
                out[pl.ds(row, devices, stride=block), :] = result[
                    part * devices : (part + 1) * devices, lanes
                ]


def finish_kernel(devices, arrived, keys, values, cotangent, *refs):
    far = refs[:4]
    near = refs[4:8]
    departures = refs[8]
    grad_queries, grad_keys, grad_values, grad_filter = near
    segment, channels = keys.shape
    parts = segment // LANES
    share = channels // devices
    block = 3 * parts * share
    copies = [
        pltpu.make_async_copy(source, target, departures.at[number])
        for number, (source, target) in enumerate(zip(near, far))
    ]

    def convolved(number, part):
        pieces = []
        for channel in range(share):
            row = (number * parts + part) * share + channel
            pieces.append(arrived[pl.ds(row, devices, stride=block), :])
        return jnp.concatenate(pieces, axis=0).T

    blocks = [pl.ds(part * LANES, LANES) for part in range(parts)]
    for part, at in enumerate(blocks):
        back_signal = convolved(1, part)
        grad_keys[at, :] = back_signal * values[at, :]
        grad_values[at, :] = back_signal * keys[at, :]
    copies[1].start()
    copies[2].start()
    for part, at in enumerate(blocks):
        grad_queries[at, :] = cotangent[at, :] * convolved(0, part)
    copies[0].start()
    for part, at in enumerate(blocks):
        grad_filter[at, :] = convolved(2, part)
    copies[3].start()
    for copy in copies:
        copy.wait()


def call(kernel, devices, out_shape, scratch=(), **specs):
    def bound(*refs):
        kernel(devices, *refs)

    return pl.pallas_call(
        bound,
        out_shape=out_shape,
        scratch_shapes=scratch,
        compiler_params=pltpu.CompilerParams(vmem_limit_bytes=VMEM_LIMIT),
        **specs,
    )


def local(queries, keys, values, cotangent, filt, skip):
    segment, channels = queries.shape
    devices = lax.axis_size(AXES)
    tokens = segment * devices
    rows = tokens // LANES
    share = channels // devices
    block = 3 * (segment // LANES) * share
    flat = pltpu.VMEM((devices * block, LANES), jnp.float32)

    group = exchange_order(lax.axis_size(AXES[0]), lax.axis_size(AXES[1]))

    def exchange(array):
        array = lax.all_to_all(
            array, AXES, split_axis=0, concat_axis=0, axis_index_groups=[group], tiled=True
        )
        return array.reshape(devices * block, LANES)

    whole = pltpu.VMEM((segment, channels), jnp.float32)
    result = jax.ShapeDtypeStruct(whole.shape, whole.dtype)
    far = pl.BlockSpec(memory_space=pltpu.HBM)
    near = pl.BlockSpec(memory_space=pltpu.VMEM)
    operands = (skip.reshape(1, channels), filt, keys, values, cotangent, queries)
    operands = tuple(pltpu.with_memory_space_constraint(array, pltpu.HBM) for array in operands)
    scratch = (pltpu.VMEM((1, channels), jnp.float32),) + (whole,) * 5 + (pltpu.SemaphoreType.DMA((6,)),)
    gate = call(gate_kernel, devices, flat, scratch, in_specs=(far,) * 6)
    arrived = exchange(gate(*operands))
    wide = pltpu.VMEM((3 * share * rows, 2 * LANES), jnp.bfloat16)
    constants = tuple(jnp.asarray(table) for table in tables(tokens, devices, group))
    convolved = call(conv_kernel, devices, flat, (wide, wide))(arrived, *constants)
    returned = exchange(convolved)
    finish = call(
        finish_kernel,
        devices,
        (result,) * 4,
        (whole,) * 4 + (pltpu.SemaphoreType.DMA((4,)),),
        in_specs=(near,) * 4,
        out_specs=(far,) * 4,
    )
    return tuple(finish(returned, keys, values, cotangent))


def solution(mesh):
    whole = P(AXES, None)
    return jax.shard_map(
        local,
        mesh=mesh,
        in_specs=(whole,) * 5 + (P(),),
        out_specs=(whole,) * 4,
        check_vma=False,
    )
```

```python
import math

import jax
import jax.numpy as jnp
import ml_dtypes
import numpy as np
from jax import lax
from jax.experimental import pallas as pl
from jax.experimental.pallas import tpu as pltpu
from jax.sharding import PartitionSpec as P

LANES = 128
AXES = ("sa", "sb")
VMEM_LIMIT = 48 * 1024 * 1024


def halves(matrix):
    high = matrix.astype(ml_dtypes.bfloat16)
    low = (matrix - high.astype(np.float64)).astype(ml_dtypes.bfloat16)
    return high, low


def exchange_order(planes, width):
    chips = width // 2
    walk = [chip for start in range(2) for chip in range(start, chips, 2)]
    places = [chip * 2 + core for chip in walk for core in range(2)]
    return [-plane % planes * width + place for place in places for plane in range(planes)]


def tables(tokens, devices, group):
    rows = tokens // LANES
    parts = rows // devices
    order = (np.array(group)[None, :] * parts + np.arange(parts)[:, None]).reshape(-1)
    half_step = np.arange(rows) + 0.5
    lane = np.arange(LANES)
    angle = 2.0 * np.pi / (2 * rows) * half_step[:, None] * order[None, :]
    first = np.concatenate([np.cos(angle), -np.sin(angle)], axis=0)
    turn_angle = 2.0 * np.pi / (2 * tokens) * half_step[:, None] * lane[None, :]
    turn = np.stack([np.cos(turn_angle), -np.sin(turn_angle)]).astype(np.float32)
    lane_angle = 2.0 * np.pi / LANES * ((lane[:, None] * lane[None, :]) % LANES)
    cosine, sine = np.cos(lane_angle), np.sin(lane_angle)
    second = np.block([[cosine, -sine], [sine, cosine]])
    factor = 1.0 / (tokens * math.sqrt(tokens))
    last = np.concatenate([np.cos(angle).T, np.sin(angle).T], axis=1) * factor
    first_high, first_low = halves(first)
    last_high, last_low = halves(last)
    second_high, second_low = halves(second)
    return (
        np.concatenate([first_high, first_high, first_low], axis=1),
        turn,
        np.stack([second_high, second_low]),
        np.concatenate([last_high, last_high, last_low], axis=1),
    )


def split(array):
    high = array.astype(jnp.bfloat16)
    low = (array - high.astype(jnp.float32)).astype(jnp.bfloat16)
    return high, low


def stacked(array):
    high, low = split(array)
    return jnp.concatenate([high, low, high], axis=0)


def matmul(left, right):
    return jnp.dot(left, right, preferred_element_type=jnp.float32)


def gate_kernel(devices, *refs):
    far = refs[:6]
    out = refs[6]
    near = refs[7:13]
    arrivals = refs[13]
    copies = [
        pltpu.make_async_copy(source, target, arrivals.at[number])
        for number, (source, target) in enumerate(zip(far, near))
    ]
    for copy in copies:
        copy.start()
    skip, filt, keys, values, cotangent, queries = near
    segment, channels = queries.shape
    parts = segment // LANES
    share = channels // devices
    block = 3 * parts * share
    for number in (1, 0, 2):
        needed = {0: (2, 3), 1: (0, 1), 2: (4, 5)}[number]
        for index in needed:
            copies[index].wait()
        if number == 1:
            first_tap = jnp.where(lax.axis_index(AXES) == 0, math.sqrt(devices * segment), 0.0)
            filt[0:1, :] += first_tap * skip[...]
        for part in range(parts):
            at = pl.ds(part * LANES, LANES)
            if number == 0:
                signal = keys[at, :] * values[at, :]
            elif number == 1:
                signal = filt[at, :]
            else:
                signal = cotangent[at, :] * queries[at, :]
            turned = signal.T
            for channel in range(share):
                row = (number * parts + part) * share + channel
                out[pl.ds(row, devices, stride=block), :] = turned[
                    channel * devices : (channel + 1) * devices, :
                ]


def conv_kernel(devices, arrived, first, turn, second, last, out, high, low):
    rows = turn.shape[1]
    parts = rows // devices
    block = arrived.shape[0] // devices
    share = block // (3 * parts)
    turn_real = turn[0]
    turn_imag = turn[1]

    def gathered(number, channel):
        pieces = []
        for part in range(parts):
            row = (number * parts + part) * share + channel
            pieces.append(arrived[pl.ds(row, devices, stride=block), :])
        return jnp.concatenate(pieces, axis=0)

    def hold(number, channel, real, imag):
        at = pl.ds((channel * 3 + number) * rows, rows)
        for value, lanes in ((real, pl.ds(0, LANES)), (imag, pl.ds(LANES, LANES))):
            high[at, lanes], low[at, lanes] = split(value)

    def lanes_transform(channel):
        at = pl.ds(channel * 3 * rows, 3 * rows)
        result = (
            matmul(high[at, :], second[0])
            + matmul(high[at, :], second[1])
            + matmul(low[at, :], second[0])
        )
        pieces = []
        for number in range(3):
            piece = result[number * rows : (number + 1) * rows]
            pieces.append((piece[:, 0:LANES], piece[:, LANES : 2 * LANES]))
        return pieces

    for number in range(3):
        signals = [stacked(gathered(number, channel)) for channel in range(share)]
        spread = matmul(first[...], jnp.concatenate(signals, axis=1))
        for channel in range(share):
            lanes = slice(channel * LANES, (channel + 1) * LANES)
            real = spread[:rows, lanes]
            imag = spread[rows:, lanes]
            hold(
                number,
                channel,
                real * turn_real - imag * turn_imag,
                real * turn_imag + imag * turn_real,
            )
    for channel in range(share):
        (gr, gi), (fr, fi), (ur, ui) = lanes_transform(channel)
        hold(0, channel, fr * gr - fi * gi, -(fr * gi + fi * gr))
        hold(1, channel, fr * ur + fi * ui, fi * ur - fr * ui)
        hold(2, channel, gr * ur + gi * ui, gi * ur - gr * ui)
    turned = [[], [], []]
    for channel in range(share):
        for number, (real, imag) in enumerate(lanes_transform(channel)):
            both = (real * turn_real - imag * turn_imag, real * turn_imag + imag * turn_real)
            turned[number].append(stacked(jnp.concatenate(both, axis=0)))
    for number in range(3):
        result = matmul(last[...], jnp.concatenate(turned[number], axis=1))
        for channel in range(share):
            lanes = slice(channel * LANES, (channel + 1) * LANES)
            for part in range(parts):
                row = (number * parts + part) * share + channel
                out[pl.ds(row, devices, stride=block), :] = result[
                    part * devices : (part + 1) * devices, lanes
                ]


def finish_kernel(devices, arrived, keys, values, cotangent, *refs):
    far = refs[:4]
    near = refs[4:8]
    departures = refs[8]
    grad_queries, grad_keys, grad_values, grad_filter = near
    segment, channels = keys.shape
    parts = segment // LANES
    share = channels // devices
    block = 3 * parts * share
    copies = [
        pltpu.make_async_copy(source, target, departures.at[number])
        for number, (source, target) in enumerate(zip(near, far))
    ]

    def convolved(number, part):
        pieces = []
        for channel in range(share):
            row = (number * parts + part) * share + channel
            pieces.append(arrived[pl.ds(row, devices, stride=block), :])
        return jnp.concatenate(pieces, axis=0).T

    blocks = [pl.ds(part * LANES, LANES) for part in range(parts)]
    for part, at in enumerate(blocks):
        back_signal = convolved(1, part)
        grad_keys[at, :] = back_signal * values[at, :]
        grad_values[at, :] = back_signal * keys[at, :]
    copies[1].start()
    copies[2].start()
    for part, at in enumerate(blocks):
        grad_queries[at, :] = cotangent[at, :] * convolved(0, part)
    copies[0].start()
    for part, at in enumerate(blocks):
        grad_filter[at, :] = convolved(2, part)
    copies[3].start()
    for copy in copies:
        copy.wait()


def call(kernel, devices, out_shape, scratch=(), **specs):
    def bound(*refs):
        kernel(devices, *refs)

    return pl.pallas_call(
        bound,
        out_shape=out_shape,
        scratch_shapes=scratch,
        compiler_params=pltpu.CompilerParams(vmem_limit_bytes=VMEM_LIMIT),
        **specs,
    )


def local(queries, keys, values, cotangent, filt, skip):
    segment, channels = queries.shape
    devices = lax.axis_size(AXES)
    tokens = segment * devices
    rows = tokens // LANES
    share = channels // devices
    block = 3 * (segment // LANES) * share
    flat = pltpu.VMEM((devices * block, LANES), jnp.float32)

    group = exchange_order(lax.axis_size(AXES[0]), lax.axis_size(AXES[1]))

    def exchange(array):
        array = lax.all_to_all(
            array, AXES, split_axis=0, concat_axis=0, axis_index_groups=[group], tiled=True
        )
        return array.reshape(devices * block, LANES)

    whole = pltpu.VMEM((segment, channels), jnp.float32)
    result = jax.ShapeDtypeStruct(whole.shape, whole.dtype)
    far = pl.BlockSpec(memory_space=pltpu.HBM)
    near = pl.BlockSpec(memory_space=pltpu.VMEM)
    operands = (skip.reshape(1, channels), filt, keys, values, cotangent, queries)
    operands = tuple(pltpu.with_memory_space_constraint(array, pltpu.HBM) for array in operands)
    scratch = (pltpu.VMEM((1, channels), jnp.float32),) + (whole,) * 5 + (pltpu.SemaphoreType.DMA((6,)),)
    gate = call(gate_kernel, devices, flat, scratch, in_specs=(far,) * 6)
    arrived = exchange(gate(*operands))
    wide = pltpu.VMEM((3 * share * rows, 2 * LANES), jnp.bfloat16)
    constants = tuple(jnp.asarray(table) for table in tables(tokens, devices, group))
    convolved = call(conv_kernel, devices, flat, (wide, wide))(arrived, *constants)
    returned = exchange(convolved)
    finish = call(
        finish_kernel,
        devices,
        (result,) * 4,
        (whole,) * 4 + (pltpu.SemaphoreType.DMA((4,)),),
        in_specs=(near,) * 4,
        out_specs=(far,) * 4,
    )
    return tuple(finish(returned, keys, values, cotangent))


def solution(mesh):
    whole = P(AXES, None)
    return jax.shard_map(
        local,
        mesh=mesh,
        in_specs=(whole,) * 5 + (P(),),
        out_specs=(whole,) * 4,
        check_vma=False,
    )
```

```python
import math

import jax
import jax.numpy as jnp
import ml_dtypes
import numpy as np
from jax import lax
from jax.experimental import pallas as pl
from jax.experimental.pallas import tpu as pltpu
from jax.sharding import PartitionSpec as P

LANES = 128
AXES = ("sa", "sb")
VMEM_LIMIT = 48 * 1024 * 1024


def halves(matrix):
    high = matrix.astype(ml_dtypes.bfloat16)
    low = (matrix - high.astype(np.float64)).astype(ml_dtypes.bfloat16)
    return high, low


def exchange_order(planes, width):
    return [
        -plane % planes * width + chip * 2 + core
        for chip in range(width // 2)
        for plane in range(planes)
        for core in range(2)
    ]


def tables(tokens, devices, group):
    rows = tokens // LANES
    parts = rows // devices
    order = (np.array(group)[None, :] * parts + np.arange(parts)[:, None]).reshape(-1)
    half_step = np.arange(rows) + 0.5
    lane = np.arange(LANES)
    angle = 2.0 * np.pi / (2 * rows) * half_step[:, None] * order[None, :]
    first = np.concatenate([np.cos(angle), -np.sin(angle)], axis=0)
    turn_angle = 2.0 * np.pi / (2 * tokens) * half_step[:, None] * lane[None, :]
    turn = np.stack([np.cos(turn_angle), -np.sin(turn_angle)]).astype(np.float32)
    lane_angle = 2.0 * np.pi / LANES * ((lane[:, None] * lane[None, :]) % LANES)
    cosine, sine = np.cos(lane_angle), np.sin(lane_angle)
    second = np.block([[cosine, -sine], [sine, cosine]])
    factor = 1.0 / (tokens * math.sqrt(tokens))
    last = np.concatenate([np.cos(angle).T, np.sin(angle).T], axis=1) * factor
    first_high, first_low = halves(first)
    last_high, last_low = halves(last)
    second_high, second_low = halves(second)
    return (
        np.concatenate([first_high, first_high, first_low], axis=1),
        turn,
        np.stack([second_high, second_low]),
        np.concatenate([last_high, last_high, last_low], axis=1),
    )


def split(array):
    high = array.astype(jnp.bfloat16)
    low = (array - high.astype(jnp.float32)).astype(jnp.bfloat16)
    return high, low


def stacked(array):
    high, low = split(array)
    return jnp.concatenate([high, low, high], axis=0)


def matmul(left, right):
    return jnp.dot(left, right, preferred_element_type=jnp.float32)


def gate_kernel(devices, *refs):
    far = refs[:6]
    out = refs[6]
    near = refs[7:13]
    arrivals = refs[13]
    copies = [
        pltpu.make_async_copy(source, target, arrivals.at[number])
        for number, (source, target) in enumerate(zip(far, near))
    ]
    for copy in copies:
        copy.start()
    skip, filt, keys, values, cotangent, queries = near
    segment, channels = queries.shape
    parts = segment // LANES
    share = channels // devices
    block = 3 * parts * share
    for number in (1, 0, 2):
        needed = {0: (2, 3), 1: (0, 1), 2: (4, 5)}[number]
        for index in needed:
            copies[index].wait()
        if number == 1:
            first_tap = jnp.where(lax.axis_index(AXES) == 0, math.sqrt(devices * segment), 0.0)
            filt[0:1, :] += first_tap * skip[...]
        for part in range(parts):
            at = pl.ds(part * LANES, LANES)
            if number == 0:
                signal = keys[at, :] * values[at, :]
            elif number == 1:
                signal = filt[at, :]
            else:
                signal = cotangent[at, :] * queries[at, :]
            turned = signal.T
            for channel in range(share):
                row = (number * parts + part) * share + channel
                out[pl.ds(row, devices, stride=block), :] = turned[
                    channel * devices : (channel + 1) * devices, :
                ]


def conv_kernel(devices, arrived, first, turn, second, last, out, high, low):
    rows = turn.shape[1]
    parts = rows // devices
    block = arrived.shape[0] // devices
    share = block // (3 * parts)
    turn_real = turn[0]
    turn_imag = turn[1]

    def gathered(number, channel):
        pieces = []
        for part in range(parts):
            row = (number * parts + part) * share + channel
            pieces.append(arrived[pl.ds(row, devices, stride=block), :])
        return jnp.concatenate(pieces, axis=0)

    def hold(number, channel, real, imag):
        at = pl.ds((channel * 3 + number) * rows, rows)
        for value, lanes in ((real, pl.ds(0, LANES)), (imag, pl.ds(LANES, LANES))):
            high[at, lanes], low[at, lanes] = split(value)

    def lanes_transform(channel):
        at = pl.ds(channel * 3 * rows, 3 * rows)
        result = (
            matmul(high[at, :], second[0])
            + matmul(high[at, :], second[1])
            + matmul(low[at, :], second[0])
        )
        pieces = []
        for number in range(3):
            piece = result[number * rows : (number + 1) * rows]
            pieces.append((piece[:, 0:LANES], piece[:, LANES : 2 * LANES]))
        return pieces

    for number in range(3):
        signals = [stacked(gathered(number, channel)) for channel in range(share)]
        spread = matmul(first[...], jnp.concatenate(signals, axis=1))
        for channel in range(share):
            lanes = slice(channel * LANES, (channel + 1) * LANES)
            real = spread[:rows, lanes]
            imag = spread[rows:, lanes]
            hold(
                number,
                channel,
                real * turn_real - imag * turn_imag,
                real * turn_imag + imag * turn_real,
            )
    for channel in range(share):
        (gr, gi), (fr, fi), (ur, ui) = lanes_transform(channel)
        hold(0, channel, fr * gr - fi * gi, -(fr * gi + fi * gr))
        hold(1, channel, fr * ur + fi * ui, fi * ur - fr * ui)
        hold(2, channel, gr * ur + gi * ui, gi * ur - gr * ui)
    turned = [[], [], []]
    for channel in range(share):
        for number, (real, imag) in enumerate(lanes_transform(channel)):
            both = (real * turn_real - imag * turn_imag, real * turn_imag + imag * turn_real)
            turned[number].append(stacked(jnp.concatenate(both, axis=0)))
    for number in range(3):
        result = matmul(last[...], jnp.concatenate(turned[number], axis=1))
        for channel in range(share):
            lanes = slice(channel * LANES, (channel + 1) * LANES)
            for part in range(parts):
                row = (number * parts + part) * share + channel
                out[pl.ds(row, devices, stride=block), :] = result[
                    part * devices : (part + 1) * devices, lanes
                ]


def finish_kernel(devices, arrived, keys, values, cotangent, *refs):
    far = refs[:4]
    near = refs[4:8]
    departures = refs[8]
    grad_queries, grad_keys, grad_values, grad_filter = near
    segment, channels = keys.shape
    parts = segment // LANES
    share = channels // devices
    block = 3 * parts * share
    copies = [
        pltpu.make_async_copy(source, target, departures.at[number])
        for number, (source, target) in enumerate(zip(near, far))
    ]

    def convolved(number, part):
        pieces = []
        for channel in range(share):
            row = (number * parts + part) * share + channel
            pieces.append(arrived[pl.ds(row, devices, stride=block), :])
        return jnp.concatenate(pieces, axis=0).T

    blocks = [pl.ds(part * LANES, LANES) for part in range(parts)]
    for part, at in enumerate(blocks):
        back_signal = convolved(1, part)
        grad_keys[at, :] = back_signal * values[at, :]
        grad_values[at, :] = back_signal * keys[at, :]
    copies[1].start()
    copies[2].start()
    for part, at in enumerate(blocks):
        grad_queries[at, :] = cotangent[at, :] * convolved(0, part)
    copies[0].start()
    for part, at in enumerate(blocks):
        grad_filter[at, :] = convolved(2, part)
    copies[3].start()
    for copy in copies:
        copy.wait()


def call(kernel, devices, out_shape, scratch=(), **specs):
    def bound(*refs):
        kernel(devices, *refs)

    return pl.pallas_call(
        bound,
        out_shape=out_shape,
        scratch_shapes=scratch,
        compiler_params=pltpu.CompilerParams(vmem_limit_bytes=VMEM_LIMIT),
        **specs,
    )


def local(queries, keys, values, cotangent, filt, skip):
    segment, channels = queries.shape
    devices = lax.axis_size(AXES)
    tokens = segment * devices
    rows = tokens // LANES
    share = channels // devices
    block = 3 * (segment // LANES) * share
    flat = pltpu.VMEM((devices * block, LANES), jnp.float32)

    group = exchange_order(lax.axis_size(AXES[0]), lax.axis_size(AXES[1]))

    def exchange(array):
        array = lax.all_to_all(
            array, AXES, split_axis=0, concat_axis=0, axis_index_groups=[group], tiled=True
        )
        return array.reshape(devices * block, LANES)

    whole = pltpu.VMEM((segment, channels), jnp.float32)
    result = jax.ShapeDtypeStruct(whole.shape, whole.dtype)
    far = pl.BlockSpec(memory_space=pltpu.HBM)
    near = pl.BlockSpec(memory_space=pltpu.VMEM)
    operands = (skip.reshape(1, channels), filt, keys, values, cotangent, queries)
    operands = tuple(pltpu.with_memory_space_constraint(array, pltpu.HBM) for array in operands)
    scratch = (pltpu.VMEM((1, channels), jnp.float32),) + (whole,) * 5 + (pltpu.SemaphoreType.DMA((6,)),)
    gate = call(gate_kernel, devices, flat, scratch, in_specs=(far,) * 6)
    arrived = exchange(gate(*operands))
    wide = pltpu.VMEM((3 * share * rows, 2 * LANES), jnp.bfloat16)
    constants = tuple(jnp.asarray(table) for table in tables(tokens, devices, group))
    convolved = call(conv_kernel, devices, flat, (wide, wide))(arrived, *constants)
    returned = exchange(convolved)
    finish = call(
        finish_kernel,
        devices,
        (result,) * 4,
        (whole,) * 4 + (pltpu.SemaphoreType.DMA((4,)),),
        in_specs=(near,) * 4,
        out_specs=(far,) * 4,
    )
    return tuple(finish(returned, keys, values, cotangent))


def solution(mesh):
    whole = P(AXES, None)
    return jax.shard_map(
        local,
        mesh=mesh,
        in_specs=(whole,) * 5 + (P(),),
        out_specs=(whole,) * 4,
        check_vma=False,
    )
```

```python
import math

import jax
import jax.numpy as jnp
import ml_dtypes
import numpy as np
from jax import lax
from jax.experimental import pallas as pl
from jax.experimental.pallas import tpu as pltpu
from jax.sharding import PartitionSpec as P

LANES = 128
AXES = ("sa", "sb")
VMEM_LIMIT = 48 * 1024 * 1024


def halves(matrix):
    high = matrix.astype(ml_dtypes.bfloat16)
    low = (matrix - high.astype(np.float64)).astype(ml_dtypes.bfloat16)
    return high, low


def exchange_order(planes, width):
    chips = width // 2
    walk = [chip ^ (chip >> 1) ^ (chips // 2) for chip in range(chips)]
    places = [chip * 2 + core for chip in walk for core in range(2)]
    return [-plane % planes * width + place for place in places for plane in range(planes)]


def tables(tokens, devices, group):
    rows = tokens // LANES
    parts = rows // devices
    order = (np.array(group)[None, :] * parts + np.arange(parts)[:, None]).reshape(-1)
    half_step = np.arange(rows) + 0.5
    lane = np.arange(LANES)
    angle = 2.0 * np.pi / (2 * rows) * half_step[:, None] * order[None, :]
    first = np.concatenate([np.cos(angle), -np.sin(angle)], axis=0)
    turn_angle = 2.0 * np.pi / (2 * tokens) * half_step[:, None] * lane[None, :]
    turn = np.stack([np.cos(turn_angle), -np.sin(turn_angle)]).astype(np.float32)
    lane_angle = 2.0 * np.pi / LANES * ((lane[:, None] * lane[None, :]) % LANES)
    cosine, sine = np.cos(lane_angle), np.sin(lane_angle)
    second = np.block([[cosine, -sine], [sine, cosine]])
    factor = 1.0 / (tokens * math.sqrt(tokens))
    last = np.concatenate([np.cos(angle).T, np.sin(angle).T], axis=1) * factor
    first_high, first_low = halves(first)
    last_high, last_low = halves(last)
    second_high, second_low = halves(second)
    return (
        np.concatenate([first_high, first_high, first_low], axis=1),
        turn,
        np.stack([second_high, second_low]),
        np.concatenate([last_high, last_high, last_low], axis=1),
    )


def split(array):
    high = array.astype(jnp.bfloat16)
    low = (array - high.astype(jnp.float32)).astype(jnp.bfloat16)
    return high, low


def stacked(array):
    high, low = split(array)
    return jnp.concatenate([high, low, high], axis=0)


def matmul(left, right):
    return jnp.dot(left, right, preferred_element_type=jnp.float32)


def gate_kernel(devices, *refs):
    far = refs[:6]
    out = refs[6]
    near = refs[7:13]
    arrivals = refs[13]
    copies = [
        pltpu.make_async_copy(source, target, arrivals.at[number])
        for number, (source, target) in enumerate(zip(far, near))
    ]
    for copy in copies:
        copy.start()
    skip, filt, keys, values, cotangent, queries = near
    segment, channels = queries.shape
    parts = segment // LANES
    share = channels // devices
    block = 3 * parts * share
    for number in (1, 0, 2):
        needed = {0: (2, 3), 1: (0, 1), 2: (4, 5)}[number]
        for index in needed:
            copies[index].wait()
        if number == 1:
            first_tap = jnp.where(lax.axis_index(AXES) == 0, math.sqrt(devices * segment), 0.0)
            filt[0:1, :] += first_tap * skip[...]
        for part in range(parts):
            at = pl.ds(part * LANES, LANES)
            if number == 0:
                signal = keys[at, :] * values[at, :]
            elif number == 1:
                signal = filt[at, :]
            else:
                signal = cotangent[at, :] * queries[at, :]
            turned = signal.T
            for channel in range(share):
                row = (number * parts + part) * share + channel
                out[pl.ds(row, devices, stride=block), :] = turned[
                    channel * devices : (channel + 1) * devices, :
                ]


def conv_kernel(devices, arrived, first, turn, second, last, out, high, low):
    rows = turn.shape[1]
    parts = rows // devices
    block = arrived.shape[0] // devices
    share = block // (3 * parts)
    turn_real = turn[0]
    turn_imag = turn[1]

    def gathered(number, channel):
        pieces = []
        for part in range(parts):
            row = (number * parts + part) * share + channel
            pieces.append(arrived[pl.ds(row, devices, stride=block), :])
        return jnp.concatenate(pieces, axis=0)

    def hold(number, channel, real, imag):
        at = pl.ds((channel * 3 + number) * rows, rows)
        for value, lanes in ((real, pl.ds(0, LANES)), (imag, pl.ds(LANES, LANES))):
            high[at, lanes], low[at, lanes] = split(value)

    def lanes_transform(channel):
        at = pl.ds(channel * 3 * rows, 3 * rows)
        result = (
            matmul(high[at, :], second[0])
            + matmul(high[at, :], second[1])
            + matmul(low[at, :], second[0])
        )
        pieces = []
        for number in range(3):
            piece = result[number * rows : (number + 1) * rows]
            pieces.append((piece[:, 0:LANES], piece[:, LANES : 2 * LANES]))
        return pieces

    for number in range(3):
        signals = [stacked(gathered(number, channel)) for channel in range(share)]
        spread = matmul(first[...], jnp.concatenate(signals, axis=1))
        for channel in range(share):
            lanes = slice(channel * LANES, (channel + 1) * LANES)
            real = spread[:rows, lanes]
            imag = spread[rows:, lanes]
            hold(
                number,
                channel,
                real * turn_real - imag * turn_imag,
                real * turn_imag + imag * turn_real,
            )
    for channel in range(share):
        (gr, gi), (fr, fi), (ur, ui) = lanes_transform(channel)
        hold(0, channel, fr * gr - fi * gi, -(fr * gi + fi * gr))
        hold(1, channel, fr * ur + fi * ui, fi * ur - fr * ui)
        hold(2, channel, gr * ur + gi * ui, gi * ur - gr * ui)
    turned = [[], [], []]
    for channel in range(share):
        for number, (real, imag) in enumerate(lanes_transform(channel)):
            both = (real * turn_real - imag * turn_imag, real * turn_imag + imag * turn_real)
            turned[number].append(stacked(jnp.concatenate(both, axis=0)))
    for number in range(3):
        result = matmul(last[...], jnp.concatenate(turned[number], axis=1))
        for channel in range(share):
            lanes = slice(channel * LANES, (channel + 1) * LANES)
            for part in range(parts):
                row = (number * parts + part) * share + channel
                out[pl.ds(row, devices, stride=block), :] = result[
                    part * devices : (part + 1) * devices, lanes
                ]


def finish_kernel(devices, arrived, keys, values, cotangent, *refs):
    far = refs[:4]
    near = refs[4:8]
    departures = refs[8]
    grad_queries, grad_keys, grad_values, grad_filter = near
    segment, channels = keys.shape
    parts = segment // LANES
    share = channels // devices
    block = 3 * parts * share
    copies = [
        pltpu.make_async_copy(source, target, departures.at[number])
        for number, (source, target) in enumerate(zip(near, far))
    ]

    def convolved(number, part):
        pieces = []
        for channel in range(share):
            row = (number * parts + part) * share + channel
            pieces.append(arrived[pl.ds(row, devices, stride=block), :])
        return jnp.concatenate(pieces, axis=0).T

    blocks = [pl.ds(part * LANES, LANES) for part in range(parts)]
    for part, at in enumerate(blocks):
        back_signal = convolved(1, part)
        grad_keys[at, :] = back_signal * values[at, :]
        grad_values[at, :] = back_signal * keys[at, :]
    copies[1].start()
    copies[2].start()
    for part, at in enumerate(blocks):
        grad_queries[at, :] = cotangent[at, :] * convolved(0, part)
    copies[0].start()
    for part, at in enumerate(blocks):
        grad_filter[at, :] = convolved(2, part)
    copies[3].start()
    for copy in copies:
        copy.wait()


def call(kernel, devices, out_shape, scratch=(), **specs):
    def bound(*refs):
        kernel(devices, *refs)

    return pl.pallas_call(
        bound,
        out_shape=out_shape,
        scratch_shapes=scratch,
        compiler_params=pltpu.CompilerParams(vmem_limit_bytes=VMEM_LIMIT),
        **specs,
    )


def local(queries, keys, values, cotangent, filt, skip):
    segment, channels = queries.shape
    devices = lax.axis_size(AXES)
    tokens = segment * devices
    rows = tokens // LANES
    share = channels // devices
    block = 3 * (segment // LANES) * share
    flat = pltpu.VMEM((devices * block, LANES), jnp.float32)

    group = exchange_order(lax.axis_size(AXES[0]), lax.axis_size(AXES[1]))

    def exchange(array):
        array = lax.all_to_all(
            array, AXES, split_axis=0, concat_axis=0, axis_index_groups=[group], tiled=True
        )
        return array.reshape(devices * block, LANES)

    whole = pltpu.VMEM((segment, channels), jnp.float32)
    result = jax.ShapeDtypeStruct(whole.shape, whole.dtype)
    far = pl.BlockSpec(memory_space=pltpu.HBM)
    near = pl.BlockSpec(memory_space=pltpu.VMEM)
    operands = (skip.reshape(1, channels), filt, keys, values, cotangent, queries)
    operands = tuple(pltpu.with_memory_space_constraint(array, pltpu.HBM) for array in operands)
    scratch = (pltpu.VMEM((1, channels), jnp.float32),) + (whole,) * 5 + (pltpu.SemaphoreType.DMA((6,)),)
    gate = call(gate_kernel, devices, flat, scratch, in_specs=(far,) * 6)
    arrived = exchange(gate(*operands))
    wide = pltpu.VMEM((3 * share * rows, 2 * LANES), jnp.bfloat16)
    constants = tuple(jnp.asarray(table) for table in tables(tokens, devices, group))
    convolved = call(conv_kernel, devices, flat, (wide, wide))(arrived, *constants)
    returned = exchange(convolved)
    finish = call(
        finish_kernel,
        devices,
        (result,) * 4,
        (whole,) * 4 + (pltpu.SemaphoreType.DMA((4,)),),
        in_specs=(near,) * 4,
        out_specs=(far,) * 4,
    )
    return tuple(finish(returned, keys, values, cotangent))


def solution(mesh):
    whole = P(AXES, None)
    return jax.shard_map(
        local,
        mesh=mesh,
        in_specs=(whole,) * 5 + (P(),),
        out_specs=(whole,) * 4,
        check_vma=False,
    )
```
